256 devices in a mesh: roll: 4 (over y), exp: 64 (over x, z, core).
Axes of the slice: x: 4, y: 4, z: 8, core: 2. Of those that a mesh axis runs over, the one named last changes fastest.
Arguments:
- tokens: bfloat16 [2048, 4096], P(('roll', 'exp')), may hold values from -6 to 6
- cotangent: bfloat16 [2048, 4096], P(('roll', 'exp')), may hold values from -6 to 6
- router_probs: bfloat16 [2048, 8], P(('roll', 'exp')), may hold values from 0.019897461 to 0.5
- expert_ids: int32 [2048, 8], P(('roll', 'exp')), may hold values from 0 to 63, all different within a row; in each aligned block of 8 rows (0 to 7, 8 to 15, ...) at most 2 rows name the same one
- rewards: int32 [64, 16], P('exp', 'roll'), may hold values from 0 to 12
- lengths: int32 [64, 16], P('exp', 'roll'), may hold values from 256 to 1024
- gate_weight: bfloat16 [64, 4096, 1536], P('exp', None, 'roll'), may hold values from -0.09375 to 0.09375
- up_weight: bfloat16 [64, 4096, 1536], P('exp', None, 'roll'), may hold values from -0.09375 to 0.09375
- down_weight: bfloat16 [64, 1536, 4096], P('exp', 'roll'), may hold values from -0.15625 to 0.15625
Outputs:
- grad_tokens: bfloat16 [2048, 4096], P(('roll', 'exp'))
- grad_probs: bfloat16 [2048, 8], P(('roll', 'exp'))
- grad_down: bfloat16 [64, 1536, 4096], P('exp', 'roll')
The draws below stay inside these ranges and needn't reach their ends.
Inputs may be any that keep to these rules, and one draw needn't show every extreme that they name: `expert_ids`: within the rows of one device no expert is named more than 2 times, a bound that some block reaches.
All inputs are finite; a program needn't handle non-finite values.
Results may differ from the reference program's by a relative error of at most 0.0065.
Values may be sent and summed in bfloat16 or wider, within the bound.
No kernel may reach another device: no remote copies, remote signals or barrier semaphores. Data moves between devices by JAX's collectives and lax.ppermute only.
A program may use at most 128 MiB of HBM per device.

```python
import math
import jax
import jax.numpy as jnp
import numpy as np
from jax import lax

D = 4096
FF = 1536
TOP = 8
GROUP = 16
TOK_ROLL = 2
EXPERTS = 64
PROMPTS = 64
ROLL_DEV = 4
TOK_DEV = 8
CAP = 2
TOKENS = 2048
N_ROLL = 4
N_EXP = 64


def draw_rewards(key, part):
    key = jax.random.fold_in(key, 7)
    level_key, value_key, pick_key = jax.random.split(key, 3)
    pick_keys = jax.random.split(pick_key, 4)
    high_prompt = jax.random.randint(pick_keys[0], (), 0, PROMPTS)
    high_member = jax.random.randint(pick_keys[1], (), GROUP - GROUP // 4, GROUP)
    low_prompt = jax.random.randint(pick_keys[2], (), 0, PROMPTS)
    low_member = jax.random.randint(pick_keys[3], (), 0, GROUP // 4)
    prompt_rows = jnp.arange(PROMPTS, dtype=jnp.int32)[:, None]
    member = jnp.arange(GROUP, dtype=jnp.int32)[None, :]
    levels = jax.random.randint(level_key, (PROMPTS, 1), 0, 4)
    levels = jnp.where(prompt_rows == high_prompt, 3, levels)
    ceiling = levels * (member * 4 // GROUP + 1) + 1
    drawn_values = jax.random.randint(value_key, (PROMPTS, GROUP), 0, 4096)
    values = drawn_values % ceiling
    values = jnp.where((prompt_rows == high_prompt) & (member == high_member), 12, values)
    values = jnp.where((prompt_rows == low_prompt) & (member == low_member), 0, values)
    return values.astype(jnp.int32)


def plant(array, key, low, high):
    longest = array.shape.index(max(array.shape))
    spots = []
    for shift in (0, 1):
        where = [jax.random.randint(jax.random.fold_in(key, axis), (), 0, length) for axis, length in enumerate(array.shape)]
        where[longest] = (where[longest] + shift) % array.shape[longest]
        spots.append(tuple(where))
    return array.at[spots[0]].set(low).at[spots[1]].set(high)


def shard_levels(rng, dims, shards, least, top_value):
    def one(dim, parts):
        draws = jax.random.uniform(jax.random.fold_in(jax.random.fold_in(rng, 6), dim), (parts,), jnp.float32, least / len(shards), top_value / len(shards))
        return jnp.repeat(jnp.exp(draws), dims[dim] // parts).reshape((-1,) + (1,) * (len(dims) - dim - 1))

    loudness = one(*shards[0])
    for cut in shards[1:]:
        loudness = loudness * one(*cut)
    return loudness


def deal_out(own_key, own, number, rows, count, top, limit, skew):
    sequence = jax.random.permutation(own_key, count)
    crowded, common = load_shares(count, rows * top, limit, skew, True), load_shares(count, rows * top, limit, skew, False)
    places = jnp.arange(count)

    def named(sizes, rotation):
        used = int((sizes > 0).sum())
        fixed = max(1, used // 4)
        shifted = fixed + (places - fixed + rotation * (used - fixed)) % max(1, count - fixed)
        return jnp.zeros((count,), jnp.int32).at[sequence[jnp.where(places < fixed, places, shifted)]].set(jnp.asarray(sizes, jnp.int32))

    sizes = jnp.where(number % 4 == 0, named(crowded, number // 4), named(common, number - number // 4 - 1))
    mixed = jax.random.permutation(jax.random.fold_in(own, 3), count)
    giver, receiver = mixed[0:count // 2 * 2:2], mixed[1:count // 2 * 2:2]
    room = jnp.minimum(sizes[giver] - 1, limit - sizes[receiver]) // 2
    room = jnp.where((giver == sequence[0]) | (receiver == sequence[0]) | (sizes[receiver] == 0), 0, jnp.maximum(room, 0))
    shifted = jax.random.randint(jax.random.fold_in(own, 4), (count // 2,), 0, 1 << 20) % (room + 1)
    sizes = sizes.at[giver].add(-shifted).at[receiver].add(shifted)
    labels = jnp.searchsorted(jnp.cumsum(sizes), jnp.arange(rows * top), side="right").astype(jnp.int32)
    table = labels.reshape(top, rows).T
    table = table[jax.random.permutation(jax.random.fold_in(own, 1), rows)]
    rotation = jax.random.randint(jax.random.fold_in(own, 2), (rows, 1), 0, top)
    return jnp.take_along_axis(table, (jnp.arange(top)[None, :] + rotation) % top, axis=1)


def load_shares(number_of, total, limit, skew, full):
    portions = [(1 << 20) // math.isqrt(grade ** skew) + 1 for grade in range(1, number_of + 1)]
    largest = limit if full else min(limit, max(-(-total // number_of), total * portions[0] // sum(portions)))
    least = 1 if total - largest >= number_of - 1 else 0
    given, rest = [largest] + [least] * (number_of - 1), total - largest - least * (number_of - 1)
    while rest > 0:
        candidates = [i for i in range(1, number_of) if given[i] < largest] or [i for i in range(1, number_of) if given[i] < limit]
        pool, budget = sum([portions[i] for i in candidates]), rest
        for i in candidates:
            addition = min(limit - given[i], max(1, budget * portions[i] // pool), rest)
            given[i] = given[i] + addition
            rest = rest - addition
    return np.array(given)


def normal_values(rng, extent, width, bound, shards=(), held_as=jnp.bfloat16):
    level = shard_levels(rng, extent, shards, -0.22, 0.18) if shards else 1.0
    array = jax.random.normal(rng, extent, jnp.float32) * width * level
    return jnp.minimum(jnp.maximum(array, -bound), bound).astype(held_as)


def setup_inputs(seed: int = 0) -> dict:
    key_of = jax.random.split(jax.random.key(seed), 10)
    tokens = normal_values(key_of[0], (TOKENS, D), 1.0, 6.0, ((0, 256),))
    cotangent = normal_values(key_of[1], (TOKENS, D), 1.0, 6.0, ((0, 256),))
    router_probs = jnp.clip(jnp.exp(math.log(0.5) - 3.224016 * jax.random.uniform(key_of[2], (TOKENS, TOP), jnp.float32) ** shard_levels(key_of[2], (TOKENS, TOP), ((0, 256),), -0.2, 0.2)), 0.019897461, 0.5).astype(jnp.bfloat16)
    expert_ids_keys = jax.random.split(jax.random.fold_in(key_of[3], 1), TOKENS // TOK_DEV)
    expert_ids_turns = jax.random.permutation(jax.random.fold_in(key_of[3], 3), TOKENS // TOK_DEV)
    expert_ids = jax.vmap(lambda own, number: deal_out(jax.random.fold_in(key_of[3], 2), own, number, TOK_DEV, EXPERTS, TOP, CAP, 2))(expert_ids_keys, expert_ids_turns).reshape((TOKENS, TOP))
    rewards = draw_rewards(jax.random.fold_in(key_of[9], 71), 0)
    lengths = plant(jax.random.randint(key_of[5], (PROMPTS, GROUP), 256, 1025), jax.random.fold_in(key_of[5], 1), 256, 1024).astype(jnp.int32)
    gate_weight = normal_values(key_of[6], (EXPERTS, D, FF), D ** -0.5, 0.09375, ((0, 64), (2, 4)))
    up_weight = normal_values(key_of[7], (EXPERTS, D, FF), D ** -0.5, 0.09375, ((0, 64), (2, 4)))
    down_weight = normal_values(key_of[8], (EXPERTS, FF, D), FF ** -0.5, 0.15625, ((0, 64), (1, 4)))
    return {"tokens": tokens, "cotangent": cotangent, "router_probs": router_probs, "expert_ids": expert_ids, "rewards": rewards, "lengths": lengths, "gate_weight": gate_weight, "up_weight": up_weight, "down_weight": down_weight}


def silu_parts(pre_value):
    sigmoid_value = jax.nn.sigmoid(pre_value)
    return (pre_value * sigmoid_value, sigmoid_value * (1.0 + pre_value * (1.0 - sigmoid_value)))

def reference(tokens, cotangent, router_probs, expert_ids, rewards, lengths, gate_weight, up_weight, down_weight):
    reward_f = rewards.astype(jnp.float32)
    length_f = lengths.astype(jnp.float32)
    totals = lax.optimization_barrier(jnp.sum(reward_f, axis=1, keepdims=True))
    squares = lax.optimization_barrier(jnp.sum(reward_f * reward_f, axis=1, keepdims=True))
    spans = lax.optimization_barrier(jnp.sum(length_f, axis=1, keepdims=True))
    mean_reward = totals / GROUP
    spread = jnp.sqrt(squares / GROUP - mean_reward * mean_reward)
    advantage = (reward_f - mean_reward) / jnp.maximum(spread, 1.0)
    weights = advantage * (spans / GROUP) / length_f
    positions = jnp.arange(TOKENS, dtype=jnp.int32)
    roll_index = positions // (TOK_DEV * N_EXP)
    prompt_index = positions // TOK_DEV % N_EXP
    member_index = roll_index * ROLL_DEV + positions % TOK_DEV // TOK_ROLL
    token_weight = weights[prompt_index, member_index]
    scaled = (token_weight[:, None] * cotangent.astype(jnp.float32)).astype(jnp.bfloat16)
    slots_total = TOKENS * TOP
    flat_ids = expert_ids.reshape(-1).astype(jnp.int32)
    ordering = jnp.argsort(flat_ids, stable=True).astype(jnp.int32)
    counts = lax.optimization_barrier(jnp.sum((flat_ids[:, None] == jnp.arange(EXPERTS, dtype=jnp.int32)[None, :]).astype(jnp.int32), axis=0))
    starts = jnp.cumsum(counts) - counts
    max_rows = N_ROLL * N_EXP * CAP
    offsets = jnp.arange(max_rows, dtype=jnp.int32)
    is_live = offsets[None, :] < counts[:, None]
    picked = jnp.minimum(starts[:, None] + offsets[None, :], slots_total - 1).astype(jnp.int32)
    assigned = jnp.where(is_live, ordering[picked], slots_total).astype(jnp.int32)
    tok_ext = jnp.concatenate([tokens, jnp.zeros((1, D), tokens.dtype)], axis=0)
    grad_ext = jnp.concatenate([scaled, jnp.zeros((1, D), scaled.dtype)], axis=0)
    prob_ext = jnp.concatenate([router_probs.reshape(-1), jnp.zeros((1,), router_probs.dtype)], axis=0)

    def one_expert(carry, inputs):
        grad_acc, prob_acc = carry
        w_gate, w_up, w_down, slot_index = inputs
        token_rows = slot_index // TOP
        rows_in = tok_ext[token_rows]
        grads_in = grad_ext[token_rows]
        probs_in = prob_ext[slot_index].astype(jnp.float32)[:, None]
        pre_gate = jnp.dot(rows_in, w_gate, preferred_element_type=jnp.float32)
        pre_up = jnp.dot(rows_in, w_up, preferred_element_type=jnp.float32)
        activated, slope = silu_parts(pre_gate)
        hidden = (activated * pre_up).astype(jnp.bfloat16)
        back_hidden = jnp.dot(grads_in, w_down.T, preferred_element_type=jnp.float32)
        hidden_grad = probs_in * back_hidden
        gate_grad = (hidden_grad * pre_up * slope).astype(jnp.bfloat16)
        up_grad = (hidden_grad * activated).astype(jnp.bfloat16)
        slot_grad = (jnp.dot(gate_grad, w_gate.T, preferred_element_type=jnp.float32) + jnp.dot(up_grad, w_up.T, preferred_element_type=jnp.float32)).astype(jnp.bfloat16)
        outputs = jnp.dot(hidden, w_down, preferred_element_type=jnp.float32)
        slot_prob = lax.optimization_barrier(jnp.sum(outputs * grads_in.astype(jnp.float32), axis=1)).astype(jnp.bfloat16)
        weighted = (probs_in * hidden.astype(jnp.float32)).astype(jnp.bfloat16)
        down_grad = jnp.dot(weighted.T, grads_in, preferred_element_type=jnp.float32).astype(jnp.bfloat16)
        grad_acc = grad_acc.at[token_rows].add(slot_grad.astype(jnp.float32))
        prob_acc = prob_acc.at[slot_index].set(slot_prob.astype(jnp.float32))
        return ((grad_acc, prob_acc), down_grad)
    start_carry = (jnp.zeros((TOKENS + 1, D), jnp.float32), jnp.zeros((slots_total + 1,), jnp.float32))
    (grad_acc, prob_acc), grad_down = lax.scan(one_expert, start_carry, (gate_weight, up_weight, down_weight, assigned))
    grad_tokens = grad_acc[:TOKENS].astype(jnp.bfloat16)
    grad_probs = prob_acc[:slots_total].reshape(TOKENS, TOP).astype(jnp.bfloat16)
    return (grad_tokens, grad_probs, grad_down)
```

```python
import jax
import jax.numpy as jnp
from jax import lax
from jax.sharding import PartitionSpec as P

BF = jnp.bfloat16
F32 = jnp.float32
META = 128
CONTRACT_LAST = (((1,), (1,)), ((), ()))
CONTRACT_FIRST = (((0,), (0,)), ((), ()))


def silu_parts(pre_value):
    sigmoid_value = jax.nn.sigmoid(pre_value)
    return (pre_value * sigmoid_value, sigmoid_value * (1.0 + pre_value * (1.0 - sigmoid_value)))


def slot_layout(ids, experts, capacity):
    tok_count, top_count = ids.shape
    chosen = (ids[..., None] == jnp.arange(experts, dtype=jnp.int32)).astype(F32)
    per_token = jnp.sum(chosen, axis=1)
    before = jnp.cumsum(per_token, axis=0) - per_token
    layout = chosen[..., None] * (
        before[:, None, :, None] == jnp.arange(capacity, dtype=F32)
    ).astype(F32)
    return layout.reshape(tok_count, top_count, experts * capacity)


def ring(n_roll, step):
    return [(i, (i + step) % n_roll) for i in range(n_roll)]


def sum_over_roll(values):
    values = values + lax.ppermute(values, "roll", [(0, 1), (1, 0), (2, 3), (3, 2)])
    return values + lax.ppermute(values, "roll", [(0, 2), (2, 0), (1, 3), (3, 1)])


def gather_roll(rows):
    up, down = ring(4, 1), ring(4, -1)
    half = rows.shape[0] // 2
    from_left = lax.ppermute(rows, "roll", up)
    from_right = lax.ppermute(rows, "roll", down)
    far = jnp.concatenate(
        [
            lax.ppermute(from_left[:half], "roll", up),
            lax.ppermute(from_right[half:], "roll", down),
        ],
        axis=0,
    )
    return [rows, from_right, far, from_left]


def scatter_roll(parts):
    up, down = ring(4, 1), ring(4, -1)
    half = parts[0].shape[0] // 2
    far = parts[2].astype(BF)
    far_a = lax.ppermute(far[:half], "roll", up)
    far_b = lax.ppermute(far[half:], "roll", down)
    next_a = jnp.concatenate([parts[1][:half] + far_a.astype(F32), parts[1][half:]], axis=0)
    next_b = jnp.concatenate([parts[3][:half], parts[3][half:] + far_b.astype(F32)], axis=0)
    got_a = lax.ppermute(next_a.astype(BF), "roll", up)
    got_b = lax.ppermute(next_b.astype(BF), "roll", down)
    return parts[0] + got_a.astype(F32) + got_b.astype(F32)


def on_device(
    tokens,
    cotangent,
    router_probs,
    expert_ids,
    rewards,
    lengths,
    gate_weight,
    up_weight,
    down_weight,
):
    experts = lax.axis_size("exp")
    n_roll = lax.axis_size("roll")
    tok_count, width = tokens.shape
    top_count = expert_ids.shape[1]
    capacity = 2
    slots = experts * capacity
    w_gate, w_up, w_down = gate_weight[0], up_weight[0], down_weight[0]

    layout = slot_layout(expert_ids, experts, capacity)
    pick = jnp.sum(layout, axis=1).astype(BF)

    def pack(rows):
        return lax.dot_general(pick, rows, CONTRACT_FIRST, preferred_element_type=F32).astype(BF)

    def exchange(rows):
        return lax.all_to_all(rows, "exp", split_axis=0, concat_axis=0, tiled=True)

    own_rows = exchange(pack(tokens))
    all_rows = lax.all_gather(own_rows, "roll", axis=0, tiled=True)

    reward_f = rewards[0].astype(F32)
    length_f = lengths[0].astype(F32)
    sums = jnp.stack([jnp.sum(reward_f), jnp.sum(reward_f * reward_f), jnp.sum(length_f)])
    totals, squares, spans = sum_over_roll(sums)
    group_size = rewards.shape[1] * n_roll
    mean_reward = totals / group_size
    spread = jnp.sqrt(squares / group_size - mean_reward * mean_reward)
    advantage = (reward_f - mean_reward) / jnp.maximum(spread, 1.0)
    weights = advantage * (spans / group_size) / length_f
    token_weight = jnp.repeat(weights, tok_count // rewards.shape[1])
    scaled = (token_weight[:, None] * cotangent.astype(F32)).astype(BF)
    meta = jnp.concatenate(
        [
            router_probs,
            expert_ids.astype(BF),
            jnp.zeros((tok_count, META - 2 * top_count), BF),
        ],
        axis=1,
    )
    grad_own = exchange(pack(jnp.concatenate([scaled, meta], axis=1)))
    grad_pieces = gather_roll(grad_own)

    pre_gate = jnp.dot(all_rows, w_gate, preferred_element_type=F32)
    pre_up = jnp.dot(all_rows, w_up, preferred_element_type=F32)
    roll_index = lax.axis_index("roll")
    my_expert = lax.axis_index("exp").astype(F32)

    def piece_of(array, d):
        return lax.dynamic_slice_in_dim(
            array, lax.rem(roll_index + d, n_roll) * slots, slots, axis=0
        )

    parts, weighted_pieces = [None] * n_roll, [None] * n_roll
    for d in (0, 1, 3, 2):
        grads = grad_pieces[d][:, :width]
        info = grad_pieces[d][:, width:].astype(F32)
        prob = jnp.sum(
            jnp.where(
                info[:, top_count : 2 * top_count] == my_expert, info[:, :top_count], 0.0
            ),
            axis=1,
            keepdims=True,
        )
        gate_d, up_d = piece_of(pre_gate, d), piece_of(pre_up, d)
        activated, slope = silu_parts(gate_d)
        hidden = (activated * up_d).astype(BF)
        back_hidden = lax.dot_general(grads, w_down, CONTRACT_LAST, preferred_element_type=F32)
        hidden_grad = prob * back_hidden
        gate_grad = (hidden_grad * up_d * slope).astype(BF)
        up_grad = (hidden_grad * activated).astype(BF)
        input_part = lax.dot_general(
            gate_grad, w_gate, CONTRACT_LAST, preferred_element_type=F32
        ) + lax.dot_general(up_grad, w_up, CONTRACT_LAST, preferred_element_type=F32)
        prob_part = jnp.sum(hidden.astype(F32) * back_hidden, axis=1, keepdims=True)
        weighted_pieces[d] = (prob * hidden.astype(F32)).astype(BF)
        parts[d] = jnp.concatenate([input_part, split_value(prob_part)], axis=1)
    own_sum = scatter_roll(parts)
    prob_sum = own_sum[:, width : width + 1] + own_sum[:, width + 1 : width + 2]
    returned = exchange(
        jnp.concatenate([own_sum[:, :width], split_value(prob_sum)], axis=1).astype(BF)
    )
    grad_tokens = lax.dot_general(
        pick, returned[:, :width], (((1,), (0,)), ((), ())), preferred_element_type=F32
    ).astype(BF)
    slot_prob = returned[:, width].astype(F32) + returned[:, width + 1].astype(F32)
    grad_probs = jnp.sum(layout * slot_prob, axis=2).astype(BF)

    down_grad = lax.dot_general(
        jnp.concatenate(weighted_pieces, axis=0),
        jnp.concatenate([piece[:, :width] for piece in grad_pieces], axis=0),
        CONTRACT_FIRST,
        preferred_element_type=F32,
    )
    return (grad_tokens, grad_probs, down_grad.astype(BF)[None])


def split_value(value):
    high = lax.reduce_precision(value, 8, 7)
    rest = (value - high).astype(BF).astype(F32)
    return jnp.concatenate(
        [high, rest, jnp.zeros((value.shape[0], META - 2), F32)], axis=1
    )


def solution(mesh):
    in_specs = (
        P(("roll", "exp"), None),
        P(("roll", "exp"), None),
        P(("roll", "exp"), None),
        P(("roll", "exp"), None),
        P("exp", "roll"),
        P("exp", "roll"),
        P("exp", None, "roll"),
        P("exp", None, "roll"),
        P("exp", "roll", None),
    )
    out_specs = (P(("roll", "exp"), None), P(("roll", "exp"), None), P("exp", "roll", None))
    return jax.shard_map(
        on_device, mesh=mesh, in_specs=in_specs, out_specs=out_specs, check_vma=False
    )
```

```python
import jax
import jax.numpy as jnp
from jax import lax
from jax.experimental import pallas as pl
from jax.experimental.pallas import tpu as pltpu
from jax.sharding import PartitionSpec as P

BF = jnp.bfloat16
F32 = jnp.float32
META = 128
N_Y = 4
CAP = 2
OUTER_BLOCK = 1024
VMEM_LIMIT = 48 * 1024 * 1024
CONTRACT_LAST = (((1,), (1,)), ((), ()))
CONTRACT_FIRST = (((0,), (0,)), ((), ()))
PLAIN = (((1,), (0,)), ((), ()))


def dot(a, b, dims=PLAIN):
    return lax.dot_general(a, b, dims, preferred_element_type=F32)


def outer_kernel(count, *refs):
    weighted = jnp.concatenate([ref[...] for ref in refs[:count]], axis=0)
    rows = jnp.concatenate([ref[...] for ref in refs[count : 2 * count]], axis=0)
    refs[-1][...] = dot(weighted, rows, CONTRACT_FIRST).astype(BF)


def outer(weighted, pieces, width):
    hidden = weighted[0].shape[1]
    return pl.pallas_call(
        lambda *refs: outer_kernel(len(pieces), *refs),
        grid=(width // OUTER_BLOCK,),
        in_specs=[pl.BlockSpec(array.shape, lambda i: (0, 0)) for array in weighted]
        + [pl.BlockSpec((piece.shape[0], OUTER_BLOCK), lambda i: (0, i)) for piece in pieces],
        out_specs=pl.BlockSpec((hidden, OUTER_BLOCK), lambda i: (0, i)),
        out_shape=jax.ShapeDtypeStruct((hidden, width), BF),
        compiler_params=pltpu.CompilerParams(vmem_limit_bytes=VMEM_LIMIT),
        name="outer",
    )(*weighted, *pieces)


def slot_layout(ids, experts):
    tok_count, top_count = ids.shape
    chosen = (ids[..., None] == jnp.arange(experts, dtype=jnp.int32)).astype(F32)
    per_token = jnp.sum(chosen, axis=1)
    before = jnp.cumsum(per_token, axis=0) - per_token
    layout = chosen[:, :, None, :] * (
        before[:, None, None, :] == jnp.arange(CAP, dtype=F32)[:, None]
    ).astype(F32)
    return layout.reshape(tok_count, top_count, CAP * experts)


def silu_parts(pre_value):
    sigmoid_value = jax.nn.sigmoid(pre_value)
    return (pre_value * sigmoid_value, sigmoid_value * (1.0 + pre_value * (1.0 - sigmoid_value)))


def split_value(value):
    high = lax.reduce_precision(value, 8, 7)
    return high, value - high


def move(rows, step):
    return lax.ppermute(rows, "roll", [(i, (i + step) % N_Y) for i in range(N_Y)])


def gather_near(rows):
    return move(rows, -1), move(rows, 1)


def gather_far(right, left):
    half = left.shape[0] // 2
    return jnp.concatenate([move(left[:half], 1), move(right[half:], -1)], axis=0)


def on_device(
    tokens,
    cotangent,
    router_probs,
    expert_ids,
    rewards,
    lengths,
    gate_weight,
    up_weight,
    down_weight,
):
    experts = lax.axis_size("exp")
    tok_count, width = tokens.shape
    top = expert_ids.shape[1]
    w_gate, w_up, w_down = gate_weight[0], up_weight[0], down_weight[0]
    my_expert = lax.axis_index("exp").astype(F32)

    layout = slot_layout(expert_ids, experts)
    pick = jnp.sum(layout, axis=1).astype(BF)

    def pack(rows):
        return dot(pick, rows, CONTRACT_FIRST).astype(BF)

    def exchange(rows):
        rows = rows.reshape(CAP, experts, rows.shape[1])
        rows = lax.all_to_all(rows, "exp", split_axis=1, concat_axis=1, tiled=True)
        return rows.reshape(CAP * experts, rows.shape[2])

    meta = [
        router_probs,
        expert_ids.astype(BF),
        jnp.zeros((tok_count, META - 2 * top), BF),
    ]
    tok_own = exchange(pack(jnp.concatenate([tokens] + meta, axis=1)))

    both = jnp.concatenate([rewards, lengths], axis=1).astype(F32)
    four = jnp.concatenate([both] + [move(both, step) for step in (1, 2, 3)], axis=0)
    members = rewards.shape[1]
    group_size = members * N_Y
    totals = jnp.sum(four[:, :members])
    squares = jnp.sum(four[:, :members] * four[:, :members])
    spans = jnp.sum(four[:, members:])
    mean_reward = totals / group_size
    spread = jnp.sqrt(squares / group_size - mean_reward * mean_reward)
    advantage = (both[0, :members] - mean_reward) / jnp.maximum(spread, 1.0)
    weights = advantage * (spans / group_size) / both[0, members:]
    token_weight = jnp.repeat(weights, tok_count // members)
    scaled = (token_weight[:, None] * cotangent.astype(F32)).astype(BF)
    tok_right, tok_left = gather_near(tok_own)
    tok_far = gather_far(tok_right, tok_left)
    grad_own = exchange(pack(scaled))
    grad_own, tok_right, tok_left = lax.optimization_barrier((grad_own, tok_right, tok_left))
    grad_right, grad_left = gather_near(grad_own)
    grad_far = gather_far(grad_right, grad_left)
    tok_own, tok_right, tok_left, tok_far = lax.optimization_barrier(
        (tok_own, tok_right, tok_left, tok_far)
    )

    lane = jnp.arange(META)

    def hidden_rows(rows, grads):
        info = rows[:, width:].astype(F32)
        prob = jnp.sum(
            jnp.where(info[:, top : 2 * top] == my_expert, info[:, :top], 0.0),
            axis=1,
            keepdims=True,
        )
        pre_gate, pre_up = dot(rows[:, :width], w_gate), dot(rows[:, :width], w_up)
        activated, slope = silu_parts(pre_gate)
        hidden = (activated * pre_up).astype(BF)
        back_hidden = dot(grads, w_down, CONTRACT_LAST)
        hidden_grad = prob * back_hidden
        gate_grad = (hidden_grad * pre_up * slope).astype(BF)
        up_grad = (hidden_grad * activated).astype(BF)
        high, rest = split_value(
            jnp.sum(hidden.astype(F32) * back_hidden, axis=1, keepdims=True)
        )
        tail = jnp.where(lane == 0, high, jnp.where(lane == 1, rest, 0.0)).astype(BF)
        return (gate_grad, up_grad, tail), (prob * hidden.astype(F32)).astype(BF)

    def input_part(gate_grad, up_grad, tail):
        part = dot(gate_grad, w_gate, CONTRACT_LAST) + dot(up_grad, w_up, CONTRACT_LAST)
        return jnp.concatenate([part.astype(BF), tail], axis=1)

    from_own, weighted_own = hidden_rows(tok_own, grad_own)
    from_right, weighted_right = hidden_rows(tok_right, grad_right)
    from_left, weighted_left = hidden_rows(tok_left, grad_left)
    from_right, from_left, grad_far = lax.optimization_barrier((from_right, from_left, grad_far))
    part_right, part_left = input_part(*from_right), input_part(*from_left)
    grad_far, part_right, part_left = lax.optimization_barrier((grad_far, part_right, part_left))
    from_far, weighted_far = hidden_rows(tok_far, grad_far)
    part_far = input_part(*from_far)
    part_own = input_part(*from_own)
    total = part_own.astype(F32)
    for rows in (move(part_right, 1), move(part_left, -1), move(part_far, 2)):
        total = total + rows.astype(F32)
    high, rest = split_value(total[:, width : width + 1] + total[:, width + 1 : width + 2])
    column = jnp.arange(width + META)
    returned = exchange(
        jnp.where(column == width, high, jnp.where(column == width + 1, rest, total)).astype(BF)
    )
    grad_tokens = dot(pick, returned[:, :width]).astype(BF)
    slot_prob = returned[:, width].astype(F32) + returned[:, width + 1].astype(F32)
    grad_probs = jnp.sum(layout * slot_prob, axis=2).astype(BF)
    down_grad = outer(
        [weighted_own, weighted_right, weighted_left, weighted_far],
        [grad_own, grad_right, grad_left, grad_far],
        width,
    )
    return (grad_tokens, grad_probs, down_grad[None])


def solution(mesh):
    in_specs = (
        P(("roll", "exp"), None),
        P(("roll", "exp"), None),
        P(("roll", "exp"), None),
        P(("roll", "exp"), None),
        P("exp", "roll"),
        P("exp", "roll"),
        P("exp", None, "roll"),
        P("exp", None, "roll"),
        P("exp", "roll", None),
    )
    out_specs = (P(("roll", "exp"), None), P(("roll", "exp"), None), P("exp", "roll", None))
    return jax.shard_map(
        on_device, mesh=mesh, in_specs=in_specs, out_specs=out_specs, check_vma=False
    )
```

```python
import jax
import jax.numpy as jnp
from jax import lax
from jax.experimental import pallas as pl
from jax.experimental.pallas import tpu as pltpu
from jax.sharding import PartitionSpec as P

BF = jnp.bfloat16
F32 = jnp.float32
META = 128
N_Y = 4
CAP = 2
OUTER_BLOCK = 1024
VMEM_LIMIT = 48 * 1024 * 1024
CONTRACT_LAST = (((1,), (1,)), ((), ()))
CONTRACT_FIRST = (((0,), (0,)), ((), ()))
PLAIN = (((1,), (0,)), ((), ()))


def dot(a, b, dims=PLAIN):
    return lax.dot_general(a, b, dims, preferred_element_type=F32)


def outer_kernel(count, *refs):
    weighted = jnp.concatenate([ref[...] for ref in refs[:count]], axis=0)
    rows = jnp.concatenate([ref[...] for ref in refs[count : 2 * count]], axis=0)
    refs[-1][...] = dot(weighted, rows, CONTRACT_FIRST).astype(BF)


def outer(weighted, pieces, width):
    hidden = weighted[0].shape[1]
    return pl.pallas_call(
        lambda *refs: outer_kernel(len(pieces), *refs),
        grid=(width // OUTER_BLOCK,),
        in_specs=[pl.BlockSpec(array.shape, lambda i: (0, 0)) for array in weighted]
        + [pl.BlockSpec((piece.shape[0], OUTER_BLOCK), lambda i: (0, i)) for piece in pieces],
        out_specs=pl.BlockSpec((hidden, OUTER_BLOCK), lambda i: (0, i)),
        out_shape=jax.ShapeDtypeStruct((hidden, width), BF),
        compiler_params=pltpu.CompilerParams(vmem_limit_bytes=VMEM_LIMIT),
        name="outer",
    )(*weighted, *pieces)


def slot_layout(ids, experts):
    tok_count, top_count = ids.shape
    chosen = (ids[..., None] == jnp.arange(experts, dtype=jnp.int32)).astype(F32)
    per_token = jnp.sum(chosen, axis=1)
    before = jnp.cumsum(per_token, axis=0) - per_token
    layout = chosen[:, :, None, :] * (
        before[:, None, None, :] == jnp.arange(CAP, dtype=F32)[:, None]
    ).astype(F32)
    return layout.reshape(tok_count, top_count, CAP * experts)


def silu_parts(pre_value):
    sigmoid_value = jax.nn.sigmoid(pre_value)
    return (pre_value * sigmoid_value, sigmoid_value * (1.0 + pre_value * (1.0 - sigmoid_value)))


def split_value(value):
    high = lax.reduce_precision(value, 8, 7)
    return high, value - high


def move(rows, step):
    return lax.ppermute(rows, "roll", [(i, (i + step) % N_Y) for i in range(N_Y)])


def gather_near(rows):
    return move(rows, -1), move(rows, 1)


def gather_far(right, left):
    half = left.shape[0] // 2
    return jnp.concatenate([move(left[:half], 1), move(right[half:], -1)], axis=0)


def on_device(
    tokens,
    cotangent,
    router_probs,
    expert_ids,
    rewards,
    lengths,
    gate_weight,
    up_weight,
    down_weight,
):
    experts = lax.axis_size("exp")
    tok_count, width = tokens.shape
    top = expert_ids.shape[1]
    w_gate, w_up, w_down = gate_weight[0], up_weight[0], down_weight[0]
    my_expert = lax.axis_index("exp").astype(F32)

    layout = slot_layout(expert_ids, experts)
    pick = jnp.sum(layout, axis=1).astype(BF)

    def pack(rows):
        return dot(pick, rows, CONTRACT_FIRST).astype(BF)

    def exchange(rows):
        rows = rows.reshape(CAP, experts, rows.shape[1])
        rows = lax.all_to_all(rows, "exp", split_axis=1, concat_axis=1, tiled=True)
        return rows.reshape(CAP * experts, rows.shape[2])

    meta = [
        router_probs,
        expert_ids.astype(BF),
        jnp.zeros((tok_count, META - 2 * top), BF),
    ]
    tok_own = exchange(pack(jnp.concatenate([tokens] + meta, axis=1)))

    both = jnp.concatenate([rewards, lengths], axis=1).astype(F32)
    four = jnp.concatenate([both] + [move(both, step) for step in (1, 2, 3)], axis=0)
    members = rewards.shape[1]
    group_size = members * N_Y
    totals = jnp.sum(four[:, :members])
    squares = jnp.sum(four[:, :members] * four[:, :members])
    spans = jnp.sum(four[:, members:])
    mean_reward = totals / group_size
    spread = jnp.sqrt(squares / group_size - mean_reward * mean_reward)
    advantage = (both[0, :members] - mean_reward) / jnp.maximum(spread, 1.0)
    weights = advantage * (spans / group_size) / both[0, members:]
    token_weight = jnp.repeat(weights, tok_count // members)
    scaled = (token_weight[:, None] * cotangent.astype(F32)).astype(BF)
    tok_right, tok_left = gather_near(tok_own)
    tok_far = gather_far(tok_right, tok_left)
    grad_own = exchange(pack(scaled))
    grad_own, tok_right, tok_left = lax.optimization_barrier((grad_own, tok_right, tok_left))
    grad_right, grad_left = gather_near(grad_own)
    grad_far = gather_far(grad_right, grad_left)
    tok_own, tok_right, tok_left, tok_far = lax.optimization_barrier(
        (tok_own, tok_right, tok_left, tok_far)
    )

    lane = jnp.arange(META)
    roll_index = lax.axis_index("roll")

    def hidden_rows(rows, grads):
        info = rows[:, width:].astype(F32)
        prob = jnp.sum(
            jnp.where(info[:, top : 2 * top] == my_expert, info[:, :top], 0.0),
            axis=1,
            keepdims=True,
        )
        pre_gate, pre_up = dot(rows[:, :width], w_gate), dot(rows[:, :width], w_up)
        activated, slope = silu_parts(pre_gate)
        hidden = (activated * pre_up).astype(BF)
        back_hidden = dot(grads, w_down, CONTRACT_LAST)
        hidden_grad = prob * back_hidden
        gate_grad = (hidden_grad * pre_up * slope).astype(BF)
        up_grad = (hidden_grad * activated).astype(BF)
        high, rest = split_value(
            jnp.sum(hidden.astype(F32) * back_hidden, axis=1, keepdims=True)
        )
        tail = jnp.where(
            lane == 2 * roll_index, high, jnp.where(lane == 2 * roll_index + 1, rest, 0.0)
        ).astype(BF)
        return (gate_grad, up_grad, tail), (prob * hidden.astype(F32)).astype(BF)

    def input_part(gate_grad, up_grad, tail):
        part = dot(gate_grad, w_gate, CONTRACT_LAST) + dot(up_grad, w_up, CONTRACT_LAST)
        return jnp.concatenate([part.astype(BF), tail], axis=1)

    from_own, weighted_own = hidden_rows(tok_own, grad_own)
    from_right, weighted_right = hidden_rows(tok_right, grad_right)
    from_left, weighted_left = hidden_rows(tok_left, grad_left)
    from_right, from_left, grad_far = lax.optimization_barrier((from_right, from_left, grad_far))
    from_far, weighted_far = hidden_rows(tok_far, grad_far)
    part_far = input_part(*from_far)
    part_far, from_right, from_left = lax.optimization_barrier((part_far, from_right, from_left))
    half = part_far.shape[0] // 2
    by_left, by_right = move(part_far[:half], 1), move(part_far[half:], -1)
    part_right, part_left = input_part(*from_right), input_part(*from_left)
    part_own = input_part(*from_own)
    to_right = (part_right[:half].astype(F32) + by_left.astype(F32)).astype(BF)
    to_left = (part_left[half:].astype(F32) + by_right.astype(F32)).astype(BF)
    first = (part_own[:half], move(to_right, 1), move(part_left[:half], -1))
    second = (part_own[half:], move(part_right[half:], 1), move(to_left, -1))
    total = [sum(rows.astype(F32) for rows in part).astype(BF) for part in (first, second)]
    returned = exchange(jnp.concatenate(total, axis=0))
    grad_tokens = dot(pick, returned[:, :width]).astype(BF)
    slot_prob = jnp.sum(returned[:, width : width + 2 * N_Y].astype(F32), axis=1)
    grad_probs = jnp.sum(layout * slot_prob, axis=2).astype(BF)
    down_grad = outer(
        [weighted_own, weighted_right, weighted_left, weighted_far],
        [grad_own, grad_right, grad_left, grad_far],
        width,
    )
    return (grad_tokens, grad_probs, down_grad[None])


def solution(mesh):
    in_specs = (
        P(("roll", "exp"), None),
        P(("roll", "exp"), None),
        P(("roll", "exp"), None),
        P(("roll", "exp"), None),
        P("exp", "roll"),
        P("exp", "roll"),
        P("exp", None, "roll"),
        P("exp", None, "roll"),
        P("exp", "roll", None),
    )
    out_specs = (P(("roll", "exp"), None), P(("roll", "exp"), None), P("exp", "roll", None))
    return jax.shard_map(
        on_device, mesh=mesh, in_specs=in_specs, out_specs=out_specs, check_vma=False
    )
```

```python
import jax
import jax.numpy as jnp
from jax import lax
from jax.experimental import pallas as pl
from jax.experimental.pallas import tpu as pltpu
from jax.sharding import PartitionSpec as P

BF = jnp.bfloat16
F32 = jnp.float32
META = 128
N_Y = 4
CAP = 2
OUTER_BLOCK = 1024
VMEM_LIMIT = 48 * 1024 * 1024
CONTRACT_LAST = (((1,), (1,)), ((), ()))
CONTRACT_FIRST = (((0,), (0,)), ((), ()))
PLAIN = (((1,), (0,)), ((), ()))


def dot(a, b, dims=PLAIN):
    return lax.dot_general(a, b, dims, preferred_element_type=F32)


def outer_kernel(count, *refs):
    weighted = jnp.concatenate([ref[...] for ref in refs[:count]], axis=0)
    rows = jnp.concatenate([ref[...] for ref in refs[count : 2 * count]], axis=0)
    refs[-1][...] = dot(weighted, rows, CONTRACT_FIRST).astype(BF)


def outer(weighted, pieces, width):
    hidden = weighted[0].shape[1]
    return pl.pallas_call(
        lambda *refs: outer_kernel(len(pieces), *refs),
        grid=(width // OUTER_BLOCK,),
        in_specs=[pl.BlockSpec(array.shape, lambda i: (0, 0)) for array in weighted]
        + [pl.BlockSpec((piece.shape[0], OUTER_BLOCK), lambda i: (0, i)) for piece in pieces],
        out_specs=pl.BlockSpec((hidden, OUTER_BLOCK), lambda i: (0, i)),
        out_shape=jax.ShapeDtypeStruct((hidden, width), BF),
        compiler_params=pltpu.CompilerParams(vmem_limit_bytes=VMEM_LIMIT),
        name="outer",
    )(*weighted, *pieces)


def slot_layout(ids, experts):
    tok_count, top_count = ids.shape
    chosen = (ids[..., None] == jnp.arange(experts, dtype=jnp.int32)).astype(F32)
    per_token = jnp.sum(chosen, axis=1)
    before = jnp.cumsum(per_token, axis=0) - per_token
    layout = chosen[:, :, None, :] * (
        before[:, None, None, :] == jnp.arange(CAP, dtype=F32)[:, None]
    ).astype(F32)
    return layout.reshape(tok_count, top_count, CAP * experts)


def silu_parts(pre_value):
    sigmoid_value = jax.nn.sigmoid(pre_value)
    return (pre_value * sigmoid_value, sigmoid_value * (1.0 + pre_value * (1.0 - sigmoid_value)))


def split_value(value):
    high = lax.reduce_precision(value, 8, 7)
    return high, value - high


def move(rows, step):
    return lax.ppermute(rows, "roll", [(i, (i + step) % N_Y) for i in range(N_Y)])


def gather_near(rows):
    return move(rows, -1), move(rows, 1)


def gather_far(right, left):
    half = left.shape[0] // 2
    return jnp.concatenate([move(left[:half], 1), move(right[half:], -1)], axis=0)


def on_device(
    tokens,
    cotangent,
    router_probs,
    expert_ids,
    rewards,
    lengths,
    gate_weight,
    up_weight,
    down_weight,
):
    experts = lax.axis_size("exp")
    tok_count, width = tokens.shape
    top = expert_ids.shape[1]
    w_gate, w_up, w_down = gate_weight[0], up_weight[0], down_weight[0]
    my_expert = lax.axis_index("exp").astype(F32)

    layout = slot_layout(expert_ids, experts)
    pick = jnp.sum(layout, axis=1).astype(BF)

    def pack(rows):
        return dot(pick, rows, CONTRACT_FIRST).astype(BF)

    def exchange(rows):
        rows = rows.reshape(CAP, experts, rows.shape[1])
        rows = lax.all_to_all(rows, "exp", split_axis=1, concat_axis=1, tiled=True)
        return rows.reshape(CAP * experts, rows.shape[2])

    meta = [
        router_probs,
        expert_ids.astype(BF),
        jnp.zeros((tok_count, META - 2 * top), BF),
    ]
    tok_own = exchange(pack(jnp.concatenate([tokens] + meta, axis=1)))

    both = jnp.concatenate([rewards, lengths], axis=1).astype(F32)
    four = jnp.concatenate([both] + [move(both, step) for step in (1, 2, 3)], axis=0)
    members = rewards.shape[1]
    group_size = members * N_Y
    totals = jnp.sum(four[:, :members])
    squares = jnp.sum(four[:, :members] * four[:, :members])
    spans = jnp.sum(four[:, members:])
    mean_reward = totals / group_size
    spread = jnp.sqrt(squares / group_size - mean_reward * mean_reward)
    advantage = (both[0, :members] - mean_reward) / jnp.maximum(spread, 1.0)
    weights = advantage * (spans / group_size) / both[0, members:]
    token_weight = jnp.repeat(weights, tok_count // members)
    scaled = (token_weight[:, None] * cotangent.astype(F32)).astype(BF)
    tok_right, tok_left = gather_near(tok_own)
    tok_far = gather_far(tok_right, tok_left)
    grad_own = exchange(pack(scaled))
    grad_own, tok_right, tok_left = lax.optimization_barrier((grad_own, tok_right, tok_left))
    grad_right, grad_left = gather_near(grad_own)
    grad_far = gather_far(grad_right, grad_left)
    tok_own, tok_right, tok_left, tok_far = lax.optimization_barrier(
        (tok_own, tok_right, tok_left, tok_far)
    )

    lane = jnp.arange(META)
    roll_index = lax.axis_index("roll")

    def hidden_rows(rows, grads):
        info = rows[:, width:].astype(F32)
        prob = jnp.sum(
            jnp.where(info[:, top : 2 * top] == my_expert, info[:, :top], 0.0),
            axis=1,
            keepdims=True,
        )
        pre_gate, pre_up = dot(rows[:, :width], w_gate), dot(rows[:, :width], w_up)
        activated, slope = silu_parts(pre_gate)
        hidden = (activated * pre_up).astype(BF)
        back_hidden = dot(grads, w_down, CONTRACT_LAST)
        hidden_grad = prob * back_hidden
        gate_grad = (hidden_grad * pre_up * slope).astype(BF)
        up_grad = (hidden_grad * activated).astype(BF)
        high, rest = split_value(
            jnp.sum(hidden.astype(F32) * back_hidden, axis=1, keepdims=True)
        )
        tail = jnp.where(
            lane == 2 * roll_index, high, jnp.where(lane == 2 * roll_index + 1, rest, 0.0)
        ).astype(BF)
        return (gate_grad, up_grad, tail), (prob * hidden.astype(F32)).astype(BF)

    def input_part(gate_grad, up_grad, tail):
        part = dot(gate_grad, w_gate, CONTRACT_LAST) + dot(up_grad, w_up, CONTRACT_LAST)
        return jnp.concatenate([part.astype(BF), tail], axis=1)

    from_own, weighted_own = hidden_rows(tok_own, grad_own)
    from_right, weighted_right = hidden_rows(tok_right, grad_right)
    from_left, weighted_left = hidden_rows(tok_left, grad_left)
    from_far, weighted_far = hidden_rows(tok_far, grad_far)
    part_far = input_part(*from_far)
    part_far, from_right, from_left = lax.optimization_barrier((part_far, from_right, from_left))
    half = part_far.shape[0] // 2
    by_left, by_right = move(part_far[:half], 1), move(part_far[half:], -1)
    part_right, part_left = input_part(*from_right), input_part(*from_left)
    part_own = input_part(*from_own)
    to_right = (part_right[:half].astype(F32) + by_left.astype(F32)).astype(BF)
    to_left = (part_left[half:].astype(F32) + by_right.astype(F32)).astype(BF)
    first = (part_own[:half], move(to_right, 1), move(part_left[:half], -1))
    second = (part_own[half:], move(part_right[half:], 1), move(to_left, -1))
    total = [sum(rows.astype(F32) for rows in part).astype(BF) for part in (first, second)]
    returned = exchange(jnp.concatenate(total, axis=0))
    grad_tokens = dot(pick, returned[:, :width]).astype(BF)
    slot_prob = jnp.sum(returned[:, width : width + 2 * N_Y].astype(F32), axis=1)
    grad_probs = jnp.sum(layout * slot_prob, axis=2).astype(BF)
    down_grad = outer(
        [weighted_own, weighted_right, weighted_left, weighted_far],
        [grad_own, grad_right, grad_left, grad_far],
        width,
    )
    return (grad_tokens, grad_probs, down_grad[None])


def solution(mesh):
    in_specs = (
        P(("roll", "exp"), None),
        P(("roll", "exp"), None),
        P(("roll", "exp"), None),
        P(("roll", "exp"), None),
        P("exp", "roll"),
        P("exp", "roll"),
        P("exp", None, "roll"),
        P("exp", None, "roll"),
        P("exp", "roll", None),
    )
    out_specs = (P(("roll", "exp"), None), P(("roll", "exp"), None), P("exp", "roll", None))
    return jax.shard_map(
        on_device, mesh=mesh, in_specs=in_specs, out_specs=out_specs, check_vma=False
    )
```
